256 devices in a mesh: grp: 16 (over z, y_lo), ep: 16 (over y_hi, x, core).
Axes of the slice: x: 4, y: 4 (y_hi: 2, y_lo: 2; y = y_hi * 2 + y_lo), z: 8, core: 2. Of those that a mesh axis runs over, the one named last changes fastest.
Arguments:
- expert_ids: int32 [2, 16384, 6], P(None, ('grp', 'ep')), may hold values from 0 to 15, all different within a row; in each aligned block of 64 rows (0 to 63, 64 to 127, ..., all dimensions but the last counted through in order) at most 32 rows name the same one
- gates: float32 [2, 16384, 6], P(None, ('grp', 'ep')), may hold values from 0.1 to 1
- hidden: bfloat16 [2, 16384, 6, 768], P(None, ('grp', 'ep')), may hold values from -4 to 4
- cotangent: bfloat16 [2, 16384, 2560], P(None, ('grp', 'ep')), may hold values from -6 to 6
- old_place: int32 [16], replicated, may hold values from 0 to 15, as said below
- new_place: int32 [16], replicated, may hold values from 0 to 15, as said below
- old_weights: bfloat16 [16, 768, 2560], P('ep'), may hold values from -0.21875 to 0.21875
Outputs:
- slot_grads: bfloat16 [2, 16384, 6, 768], P(None, ('grp', 'ep'))
- new_weights: bfloat16 [16, 768, 2560], P('ep')
- expert_grads: bfloat16 [16, 768, 2560], P('ep', None, 'grp')
The draws below stay inside these ranges and needn't reach their ends.
Inputs may be any that keep to these rules, and one draw needn't show every extreme that they name: `expert_ids`: each row names 6 different experts; within one micro-batch no expert is named by more than 32 of the 64 tokens of one device, and some expert reaches 32. A permutation of the slots: expert e sits in slot old_place[e]. A permutation of the slots: expert e sits in slot new_place[e].
All inputs are finite; a program needn't handle non-finite values.
Results may differ from the reference program's by a relative error of at most 0.024.
Values may be sent and summed in bfloat16 or wider, within the bound.
A program may use at most 128 MiB of HBM per device.

```python
import math
import jax
import jax.numpy as jnp
import numpy as np
from jax import lax

D = 2560
H = 768
TOP = 6
MB = 2
T_MB = 64
E_DEV = 1
EXPERTS = 16
CAP = 32
TOKENS = 16384
N_GRP = 16
N_EP = 16


def placement_pair(key):
    old_slots = jax.random.permutation(jax.random.fold_in(key, 11), EXPERTS).astype(jnp.int32)
    ep_count = EXPERTS // E_DEV
    first = jax.random.randint(jax.random.fold_in(key, 12), (), 0, EXPERTS).astype(jnp.int32)
    second = (first + E_DEV) % EXPERTS
    third = (second + ep_count // 2 * E_DEV) % EXPERTS
    mapping = jnp.arange(EXPERTS, dtype=jnp.int32)
    mapping = mapping.at[first].set(second).at[second].set(third).at[third].set(first)
    new_slots = jnp.take(mapping, old_slots, axis=0).astype(jnp.int32)
    return (old_slots, new_slots)


def draw_old_place(key, part):
    return placement_pair(key)[0]


def draw_new_place(key, part):
    return placement_pair(key)[1]


def block_scale(stream_key, shape, split, smallest, top_value):
    factor_of = 1.0
    for dim, parts in split:
        draws = jax.random.uniform(jax.random.fold_in(jax.random.fold_in(stream_key, 6), dim), (parts,), jnp.float32, smallest / len(split), top_value / len(split))
        factor_of = factor_of * jnp.repeat(jnp.exp(draws), shape[dim] // parts).reshape((-1,) + (1,) * (len(shape) - 1 - dim))
    return factor_of


def assign_block(own_key, own, number, rows, amount, top, bound, slope):
    order = jax.random.permutation(own_key, amount)
    crowded, common = shares(amount, rows * top, bound, slope, True), shares(amount, rows * top, bound, slope, False)
    places = jnp.arange(amount)

    def named(lengths, rotation):
        used = int((lengths > 0).sum())
        fixed = max(1, used // 4)
        shifted = fixed + (places - fixed + rotation * (used - fixed)) % max(1, amount - fixed)
        return jnp.zeros((amount,), jnp.int32).at[order[jnp.where(places < fixed, places, shifted)]].set(jnp.asarray(lengths, jnp.int32))

    lengths = jnp.where(number % 4 == 0, named(crowded, number // 4), named(common, number - number // 4 - 1))
    mixed = jax.random.permutation(jax.random.fold_in(own, 3), amount)
    donor, receiver = mixed[0:amount // 2 * 2:2], mixed[1:amount // 2 * 2:2]
    slack = jnp.minimum(lengths[donor] - 1, bound - lengths[receiver]) // 2
    slack = jnp.where((donor == order[0]) | (receiver == order[0]) | (lengths[receiver] == 0), 0, jnp.maximum(slack, 0))
    shifted = jax.random.randint(jax.random.fold_in(own, 4), (amount // 2,), 0, 1 << 20) % (slack + 1)
    lengths = lengths.at[donor].add(-shifted).at[receiver].add(shifted)
    labels = jnp.searchsorted(jnp.cumsum(lengths), jnp.arange(rows * top), side="right").astype(jnp.int32)
    table = labels.reshape(top, rows).T
    table = table[jax.random.permutation(jax.random.fold_in(own, 1), rows)]
    rotation = jax.random.randint(jax.random.fold_in(own, 2), (rows, 1), 0, top)
    return jnp.take_along_axis(table, (jnp.arange(top)[None, :] + rotation) % top, axis=1)


def shares(count, total, limit, lean, full):
    portions = [(1 << 20) // math.isqrt(grade ** lean) + 1 for grade in range(1, count + 1)]
    largest = limit if full else min(limit, max(-(-total // count), total * portions[0] // sum(portions)))
    least = 1 if total - largest >= count - 1 else 0
    given, rest = [largest] + [least] * (count - 1), total - largest - least * (count - 1)
    while rest > 0:
        free = [i for i in range(1, count) if given[i] < largest] or [i for i in range(1, count) if given[i] < limit]
        pool, left = sum([portions[i] for i in free]), rest
        for i in free:
            addition = min(limit - given[i], max(1, left * portions[i] // pool), rest)
            given[i] = given[i] + addition
            rest = rest - addition
    return np.array(given)


def scatter_about(key, extent, width, reach, split=(), kind=jnp.bfloat16):
    result = jax.random.normal(key, extent, jnp.float32) * width
    if len(split) > 0:
        result = block_scale(key, extent, split, -0.22, 0.18) * result
    return jnp.clip(result, min=-reach, max=reach).astype(kind)


def setup_inputs(seed: int = 0) -> dict:
    key_of = jax.random.split(jax.random.key(seed), 8)
    expert_ids_keys = jax.random.split(jax.random.fold_in(key_of[0], 1), MB * TOKENS // T_MB)
    expert_ids_turns = jax.random.permutation(jax.random.fold_in(key_of[0], 3), MB * TOKENS // T_MB)
    expert_ids = jax.vmap(lambda own, number: assign_block(jax.random.fold_in(key_of[0], 2), own, number, T_MB, EXPERTS, TOP, CAP, 2))(expert_ids_keys, expert_ids_turns).reshape((MB, TOKENS, TOP))
    gates = jnp.clip(jnp.exp(math.log(1.0) - 2.3025851 * jax.random.uniform(key_of[1], (MB, TOKENS, TOP), jnp.float32) ** block_scale(key_of[1], (MB, TOKENS, TOP), ((1, 256),), -0.2, 0.2)), 0.1, 1.0)
    hidden = scatter_about(key_of[2], (MB, TOKENS, TOP, H), 0.5, 4.0, ((1, 256),))
    cotangent = scatter_about(key_of[3], (MB, TOKENS, D), 1.0, 6.0, ((1, 256),))
    old_place = draw_old_place(jax.random.fold_in(key_of[7], 71), 0)
    new_place = draw_new_place(jax.random.fold_in(key_of[7], 71), 0)
    old_weights = scatter_about(key_of[6], (EXPERTS, H, D), H ** -0.5, 0.21875, ((0, 16),))
    return dict(expert_ids=expert_ids, gates=gates, hidden=hidden, cotangent=cotangent, old_place=old_place, new_place=new_place, old_weights=old_weights)


def group_pass(routed, gate_rows, hid_rows, cot_rows, weights):
    flat_ids = routed.reshape(-1)
    numbers = jnp.arange(EXPERTS, dtype=jnp.int32)
    onehot = (flat_ids[:, None] == numbers[None, :]).astype(jnp.int32)
    before = jnp.cumsum(onehot, axis=0) - onehot
    position = jnp.sum(before * onehot, axis=1)
    depth = N_EP * CAP
    buffer_rows = (flat_ids * depth + position).astype(jnp.int32)
    scaled = (gate_rows[:, :, None] * cot_rows[:, None, :].astype(jnp.float32)).astype(jnp.bfloat16)
    scaled = scaled.reshape(-1, D)
    scaled_buf = jnp.zeros((EXPERTS * depth, D), jnp.bfloat16).at[buffer_rows].set(scaled)
    scaled_buf = scaled_buf.reshape(EXPERTS, depth, D)
    hid_buf = jnp.zeros((EXPERTS * depth, H), jnp.bfloat16).at[buffer_rows].set(hid_rows.reshape(-1, H))
    hid_buf = hid_buf.reshape(EXPERTS, depth, H)
    back_buf = jnp.einsum("erd,ehd->erh", scaled_buf.astype(jnp.float32), weights.astype(jnp.float32))
    back_buf = back_buf.astype(jnp.bfloat16).reshape(-1, H)
    slot_back = jnp.take(back_buf, buffer_rows, axis=0).reshape(routed.shape + (H,))
    partial_value = jnp.einsum("erh,erd->ehd", hid_buf.astype(jnp.float32), scaled_buf.astype(jnp.float32))
    return slot_back, partial_value.astype(jnp.bfloat16)


def reference(expert_ids, gates, hidden, cotangent, old_place, new_place, old_weights):
    weights = jnp.take(old_weights, old_place, axis=0)
    new_weights = jnp.zeros_like(old_weights).at[new_place].set(weights)
    group_tokens = T_MB * N_EP
    rounded = []
    slot_list = []
    for batch in range(MB):
        routed = expert_ids[batch].reshape(N_GRP, group_tokens, TOP)
        gate_part = gates[batch].reshape(N_GRP, group_tokens, TOP)
        hid_part = hidden[batch].reshape(N_GRP, group_tokens, TOP, H)
        cot_part = cotangent[batch].reshape(N_GRP, group_tokens, D)

        def scan_step(carry, pieces):
            slot_back, partial_value = group_pass(pieces[0], pieces[1], pieces[2], pieces[3], weights)
            widened = lax.optimization_barrier(partial_value).astype(jnp.float32)
            return carry + widened, slot_back

        zero_sum = jnp.zeros((EXPERTS, H, D), jnp.float32)
        summed, slot_back = lax.scan(scan_step, zero_sum, (routed, gate_part, hid_part, cot_part))
        slot_list.append(slot_back.reshape(TOKENS, TOP, H))
        rounded.append(lax.optimization_barrier(summed.astype(jnp.bfloat16)).astype(jnp.float32))
    merged = ((rounded[0] + rounded[1]) / N_GRP).astype(jnp.bfloat16)
    expert_grads = jnp.zeros_like(old_weights).at[new_place].set(merged)
    return jnp.stack(slot_list), new_weights, expert_grads
```

```python
import jax
import jax.numpy as jnp
from jax import lax
from jax.sharding import PartitionSpec as P

F32 = jnp.float32
BF16 = jnp.bfloat16


def local(expert_ids, gates, hidden, cotangent, old_place, new_place, old_weights):
    ep_count = lax.axis_size("ep")
    grp_count = lax.axis_size("grp")
    width_h, width_d = old_weights.shape[1:]
    experts = old_place.shape[0]
    micros, toks, tops = expert_ids.shape
    cap = min(toks, 32)
    ep_rank = lax.axis_index("ep")
    grp_rank = lax.axis_index("grp")
    share = width_d // grp_count
    numbers = jnp.arange(experts, dtype=jnp.int32)

    eq = expert_ids[..., None] == numbers
    routed = jnp.any(eq, axis=2)
    tri = (jnp.arange(toks)[:, None] > jnp.arange(toks)[None, :]).astype(F32)
    rank = jnp.einsum("tu,mue->mte", tri, routed.astype(F32)).astype(jnp.int32)
    slot_rank = jnp.sum(jnp.where(eq, rank[:, :, None, :], 0), axis=-1)
    row_old = jnp.sum(jnp.where(eq, old_place, 0), axis=-1) * cap + slot_rank
    row_new = jnp.sum(jnp.where(eq, new_place, 0), axis=-1) * cap + slot_rank
    coded = jnp.where(routed, rank, -1).astype(F32)
    at_old = (old_place[:, None] == numbers[None, :]).astype(F32)
    at_new = (new_place[:, None] == numbers[None, :]).astype(F32)
    meta = jnp.concatenate([coded @ at_old, coded @ at_new], axis=-1).astype(BF16)

    my_share = lax.dynamic_slice_in_dim(old_weights[0], grp_rank * share, share, 1).T
    shares = lax.all_gather(my_share, "ep")
    source = jnp.sum(jnp.where(new_place == ep_rank, old_place, 0))
    picked = lax.dynamic_index_in_dim(shares, source, 0, keepdims=False)
    new_weights = lax.all_gather(picked, "grp", tiled=True).T[None]

    gated = (hidden.astype(F32) * gates[..., None]).astype(BF16).reshape(micros, toks * tops, width_h)
    rows = jnp.arange(ep_count * cap)
    put = (rows[None, :, None] == row_new.reshape(micros, 1, -1)).astype(BF16)
    hid_out = jnp.einsum("mrs,msh->mrh", put, gated, preferred_element_type=F32).astype(BF16)
    hid_out = hid_out.reshape(micros, ep_count, cap, width_h).transpose(1, 0, 2, 3)

    meta_all = lax.all_gather(meta, "ep")
    cot_all = lax.all_gather(cotangent, "ep")
    hid_in = lax.all_to_all(hid_out, "ep", split_axis=0, concat_axis=0, tiled=True)

    places = jnp.arange(cap).astype(BF16)
    pick_old = lax.dynamic_index_in_dim(meta_all, ep_rank, 3) == places
    pick_new = lax.dynamic_index_in_dim(meta_all, experts + ep_rank, 3) == places
    hid_rows = jnp.einsum(
        "smtp,smph->smth", pick_new.astype(BF16), hid_in, preferred_element_type=F32
    ).astype(BF16)
    cot_rows = cot_all.reshape(-1, width_d)
    part = lax.dot_general(
        cot_rows, hid_rows.reshape(-1, width_h), (((0,), (0,)), ((), ())), preferred_element_type=F32
    ).astype(BF16)
    summed = lax.psum_scatter(part, "grp", scatter_dimension=0, tiled=True)

    back = lax.dot_general(
        cot_rows, old_weights[0], (((1,), (1,)), ((), ())), preferred_element_type=F32
    ).astype(BF16)
    back = jnp.einsum(
        "smtp,smth->smph",
        pick_old.astype(BF16),
        back.reshape(ep_count, micros, toks, width_h),
        preferred_element_type=F32,
    ).astype(BF16)
    returned = lax.all_to_all(back, "ep", split_axis=0, concat_axis=0, tiled=True)
    returned = returned.transpose(1, 0, 2, 3).reshape(micros, ep_count * cap, width_h)
    get = (rows[None, None, :] == row_old.reshape(micros, -1, 1)).astype(BF16)
    got = jnp.einsum("msr,mrh->msh", get, returned, preferred_element_type=F32)
    slot_grads = (got.reshape(micros, toks, tops, width_h) * gates[..., None]).astype(BF16)

    expert_grads = (summed.astype(F32) / grp_count).astype(BF16).T[None]
    return slot_grads, new_weights, expert_grads


def solution(mesh):
    in_specs = (
        P(None, ("grp", "ep"), None),
        P(None, ("grp", "ep"), None),
        P(None, ("grp", "ep"), None, None),
        P(None, ("grp", "ep"), None),
        P(),
        P(),
        P("ep", None, None),
    )
    out_specs = (P(None, ("grp", "ep"), None, None), P("ep", None, None), P("ep", None, "grp"))
    return jax.shard_map(local, mesh=mesh, in_specs=in_specs, out_specs=out_specs, check_vma=False)
```

```python
import functools

import jax
import jax.numpy as jnp
from jax import lax
from jax.experimental import pallas as pl
from jax.experimental.pallas import tpu as pltpu
from jax.sharding import PartitionSpec as P

F32 = jnp.float32
BF16 = jnp.bfloat16
MESH = pl.DeviceIdType.MESH

CHUNKS = 5
PIECES = 17
CAP = 32


def dot(a, b, ca, cb):
    return lax.dot_general(a, b, (((ca,), (cb,)), ((), ())), preferred_element_type=F32)


def kernel(
    ids, gates, old_place, new_place, hid, cot, w_old, sg_out, w_out, eg_out,
    gat, wsh, w_res, w_perm, cot_v, hid_v, a_mat, hid_send, hid_in, hid_rows, acc,
    meta_send, meta_in, ret_send, ret_in, part, rs_r0, rs_l0, rs_r, rs_l, ysend, yrecv, eg_sum,
    w_own, sg_v,
    loc, ag_s, ag_r, hid_s, hid_r, meta_s, meta_r, ret_s, ret_r, z_s, z_r, zy_s, zy_r, c_s, c_r, cy_s, cy_r,
):
    g = lax.axis_index("grp")
    me = lax.axis_index("ep")
    z, yl = g // 2, g % 2
    core, xx, yh = me % 2, (me // 2) % 4, me // 8
    share = w_own.shape[0]
    ep_n = 16
    width_h = hid_v.shape[-1]

    def at_ep(dy=0, dx=0, dc=0):
        return (((yh + dy) % 2) * 4 + (xx + dx + 4) % 4) * 2 + (core + dc) % 2

    def to_ep(e):
        return (g, e)

    zp, zm = (((z + 1) % 8) * 2 + yl, me), (((z + 7) % 8) * 2 + yl, me)
    yp = (z * 2 + 1 - yl, me)
    left, right, yside, other = at_ep(dx=-1), at_ep(dx=1), at_ep(dy=1), at_ep(dc=1)

    def rdma(src, dst, ss, rs, dev):
        return pltpu.make_async_remote_copy(
            src_ref=src, dst_ref=dst, send_sem=ss, recv_sem=rs, device_id=dev, device_id_type=MESH
        )

    barrier = pltpu.get_barrier_semaphore()
    for d in range(1, ep_n):
        pl.semaphore_signal(barrier, 1, device_id=to_ep((me + d) % ep_n), device_id_type=MESH)
    for dev in (zp, zm, yp):
        pl.semaphore_signal(barrier, 1, device_id=dev, device_id_type=MESH)

    loads = [pltpu.make_async_copy(cot, cot_v, loc.at[0]), pltpu.make_async_copy(w_old, w_res, loc.at[1])]
    loads += [pltpu.make_async_copy(hid.at[:, k], hid_v.at[k], loc.at[2 + k]) for k in range(6)]
    my_rows = pl.ds(pl.multiple_of(g * share, 16), share)
    loads.append(pltpu.make_async_copy(w_old.at[my_rows], wsh.at[me], loc.at[8]))
    for cp in loads:
        cp.start()
    pl.semaphore_wait(barrier, ep_n - 1 + 3)

    def block(job, src):
        if job is None:
            return wsh.at[src]
        return gat.at[job, src]

    def half(job, src, h):
        if job is None:
            n = wsh.shape[2] // 2
            return wsh.at[src, :, pl.ds(h * n, n)]
        n = gat.shape[2] // 2
        return gat.at[job, src, pl.ds(h * n, n)]

    def ag_send(job, piece, ref, dev, src=None):
        j = 0 if job is None else job + 1
        rdma(ref if src is None else src, ref, ag_s.at[j, piece], ag_r.at[j, piece], to_ep(dev)).start()

    def ag_wait(job, piece, ref):
        j = 0 if job is None else job + 1
        rdma(ref, ref, ag_s.at[j, piece], ag_r.at[j, piece], to_ep(other)).wait_recv()

    def ag0(job):
        own = block(job, me)
        src = w_old.at[my_rows] if job is None else None
        ag_send(job, 0, own, right, src)
        ag_send(job, 1, own, left, src)
        ag_send(job, 2, own, yside, src)
        ag_send(job, 3, own, other, src)

    x2 = at_ep(dx=2)
    yleft, yright, yx2 = at_ep(dy=1, dx=-1), at_ep(dy=1, dx=1), at_ep(dy=1, dx=2)

    def ag1(job):
        ag_wait(job, 0, block(job, left))
        ag_send(job, 4, half(job, left, 0), right)
        ag_send(job, 10, block(job, left), other)
        ag_wait(job, 1, block(job, right))
        ag_send(job, 5, half(job, right, 1), left)
        ag_send(job, 11, block(job, right), other)
        ag_wait(job, 2, block(job, yside))
        ag_send(job, 6, block(job, yside), right)
        ag_send(job, 7, block(job, yside), left)
        ag_send(job, 12, block(job, yside), other)

    def ag2(job):
        ag_wait(job, 4, half(job, x2, 0))
        ag_send(job, 8, half(job, x2, 0), yside)
        ag_wait(job, 5, half(job, x2, 1))
        ag_send(job, 9, half(job, x2, 1), yside)
        ag_send(job, 13, block(job, x2), other)
        ag_wait(job, 6, block(job, yleft))
        ag_send(job, 14, block(job, yleft), other)
        ag_wait(job, 7, block(job, yright))
        ag_send(job, 15, block(job, yright), other)

    def ag3(job):
        ag_wait(job, 8, half(job, yx2, 0))
        ag_wait(job, 9, half(job, yx2, 1))
        ag_send(job, 16, block(job, yx2), other)

    def across(e):
        return (e // 2) * 2 + 1 - core

    def ag4(job):
        for piece, src in ((3, me), (10, left), (11, right), (12, yside), (13, x2), (14, yleft), (15, yright), (16, yx2)):
            ag_wait(job, piece, block(job, across(src)))

    def ag_drain(job):
        for piece in range(PIECES):
            ref = half(job, me, 0) if piece in (4, 5, 8, 9) else block(job, me)
            j = 0 if job is None else job + 1
            rdma(ref, ref, ag_s.at[j, piece], ag_r.at[j, piece], to_ep(other)).wait_send()

    ag0(None)

    lane = lax.broadcasted_iota(jnp.int32, (16, 128), 1)
    row16 = lax.broadcasted_iota(jnp.int32, (16, 128), 0)
    micro = (lane[:1] >= 64).astype(F32)
    ui = lax.broadcasted_iota(jnp.int32, (128, 128), 0)
    uj = lax.broadcasted_iota(jnp.int32, (128, 128), 1)
    upper = ((ui < uj) & ((ui >= 64) == (uj >= 64))).astype(BF16)
    slot_of = [jnp.zeros((16, 128), F32), jnp.zeros((16, 128), F32)]
    source = jnp.int32(0)
    for e in range(16):
        slot_of[0] = jnp.where(row16 == e, old_place[e].astype(F32), slot_of[0])
        slot_of[1] = jnp.where(row16 == e, new_place[e].astype(F32), slot_of[1])
        source = source + jnp.where(new_place[e] == me, old_place[e], 0)
    target = [[], []]
    for which in (0, 1):
        slots, hits = [], []
        for k in range(6):
            eq = ids[k : k + 1, :] == row16
            slot = jnp.sum(jnp.where(eq, slot_of[which], 0.0), axis=0, keepdims=True)
            slots.append(slot)
            hits.append(row16.astype(F32) == slot)
        routed = sum(h.astype(F32) for h in hits)
        rank = dot(routed.astype(BF16), upper, 1, 0)
        for k in range(6):
            mine = jnp.sum(jnp.where(hits[k], rank, 0.0), axis=0, keepdims=True)
            target[which].append(slots[k] * (2 * CAP) + micro * CAP + mine)
        coded = jnp.where(routed > 0.5, rank + micro * CAP, -1.0)
        for s in range(16):
            meta_send[s, which : which + 1, :] = coded[s : s + 1, :]

    def build(which):
        rows = lax.broadcasted_iota(jnp.int32, (1024, 128), 0).astype(F32)
        for k in range(6):
            a_mat[:, k * 128 : (k + 1) * 128] = jnp.where(
                rows == target[which][k], gates[k : k + 1, :], 0.0
            ).astype(BF16)

    def spread_out(src, dst, ss, rs):
        for d in range(1, ep_n):
            e = (me + d) % ep_n
            rdma(src.at[e], dst.at[me], ss.at[d], rs.at[d], to_ep(e)).start()

    def spread_wait(dst, ss, rs):
        for d in range(1, ep_n):
            e = (me - d + ep_n) % ep_n
            rdma(dst.at[e], dst.at[e], ss.at[d], rs.at[d], to_ep(other)).wait_recv()

    def spread_drain(src, ss, rs):
        for d in range(1, ep_n):
            rdma(src.at[me], src.at[me], ss.at[d], rs.at[d], to_ep(other)).wait_send()

    spread_out(meta_send, meta_in, meta_s, meta_r)
    meta_in[me] = meta_send[me]

    build(1)
    for cp in loads[2:8]:
        cp.wait()
    hid_all = hid_v[...].reshape(6 * 128, width_h)

    def pack(i, _):
        rows = pl.ds(pl.multiple_of(i * 256, 256), 256)
        res = dot(a_mat[rows, :], hid_v[...].reshape(6 * 128, width_h), 1, 0).astype(BF16)
        hid_send[pl.ds(i * 4, 4)] = res.reshape(4, 64, width_h)
        return 0

    lax.fori_loop(0, 4, pack, 0)
    spread_out(hid_send, hid_in, hid_s, hid_r)
    hid_in[me] = hid_send[me]

    def chooser(c):
        i = lax.broadcasted_iota(jnp.int32, (640, 128), 0)
        j = lax.broadcasted_iota(jnp.int32, (640, 128), 1)
        return (i == (j // 32) * 160 + c * 32 + j % 32).astype(BF16)

    loads[0].wait()

    def perm_cot(c, _):
        sel = chooser(c)
        for q in range(4):
            gat[c, me, :, q * 128 : (q + 1) * 128] = dot(
                cot_v[:, q * 640 : (q + 1) * 640], sel, 1, 0
            ).astype(BF16)
        return 0

    lax.fori_loop(0, CHUNKS, perm_cot, 0)
    ag0(0)
    ag1(None)
    loads[1].wait()

    def perm_w(c, _):
        sel = chooser(c)
        for q in range(4):
            w_perm[c, :, q * 128 : (q + 1) * 128] = dot(
                w_res[:, q * 640 : (q + 1) * 640], sel, 1, 0
            ).astype(BF16)
        return 0

    lax.fori_loop(0, 2, perm_w, 0)
    ag2(None)
    lax.fori_loop(2, CHUNKS, perm_w, 0)
    ag3(None)
    loads[8].wait()
    ag4(None)

    def w_rows(zz, yy):
        return w_out.at[pl.ds(pl.multiple_of(((zz + 16) % 8 * 2 + yy) * share, 16), share)]

    def z_send(ref, dst, way, step, yy):
        rdma(ref, dst, z_s.at[way, step, yy], z_r.at[way, step, yy], zp if way == 0 else zm).start()

    def z_wait(ref, way, step, yy):
        rdma(ref, ref, z_s.at[way, step, yy], z_r.at[way, step, yy], zp).wait_recv()

    w_own[...] = wsh[source]
    keep_own = pltpu.make_async_copy(w_own, w_rows(z, yl), loc.at[9])
    keep_own.start()
    for way in (0, 1):
        z_send(w_own, w_rows(z, yl), way, 0, yl)
    rdma(w_own, w_rows(z, yl), zy_s.at[0], zy_r.at[0], yp).start()

    def zag(step):
        if step == 0:
            ref = w_rows(z, 1 - yl)
            rdma(ref, ref, zy_s.at[0], zy_r.at[0], yp).wait_recv()
            for way in (0, 1):
                z_send(ref, ref, way, 0, 1 - yl)
            return
        for way in (0, 1):
            zz = z - step if way == 0 else z + step
            for yy in (0, 1):
                ref = w_rows(zz, yy)
                if step < 4 or yy == way:
                    z_wait(ref, way, step - 1, yy)
                if step < 3 or (step == 3 and yy == way):
                    z_send(ref, ref, way, step, yy)

    def c_rows(c, zz, h=None):
        start = pl.multiple_of(((zz + 16) % 8) * 64 + (0 if h is None else h * 32), 32)
        return part.at[c, pl.ds(start, 64 if h is None else 32)]

    def add_into(ref, other_ref):
        ref[...] = (ref[...].astype(F32) + other_ref[...].astype(F32)).astype(BF16)

    def rs_move(c, step, way, src, dst):
        return rdma(src, dst, c_s.at[c, step, way], c_r.at[c, step, way], zp if way == 0 else zm)

    def rs(c, step):
        if step == 0:
            rs_move(c, 0, 0, c_rows(c, z + 4, 0), rs_r0.at[c]).start()
            rs_move(c, 0, 1, c_rows(c, z - 4, 1), rs_l0.at[c]).start()
            return
        if step == 5:
            rdma(yrecv.at[c], yrecv.at[c], cy_s.at[c], cy_r.at[c], yp).wait_recv()
            tot = eg_sum[c] + yrecv[c].astype(F32)
            eg_out[pl.ds(pl.multiple_of(c * 32, 32), 32), :] = (tot / 16.0).astype(BF16)
            return
        if step == 4:
            rs_move(c, 3, 0, rs_r.at[c, 2], rs_r.at[c, 2]).wait_recv()
            rs_move(c, 3, 1, rs_l.at[c, 2], rs_l.at[c, 2]).wait_recv()
            for h in (0, 1):
                rows = pl.ds(h * 32, 32)
                tot = (
                    c_rows(c, z, h)[...].astype(F32)
                    + rs_r[c, 2, rows, :].astype(F32)
                    + rs_l[c, 2, rows, :].astype(F32)
                )

                @pl.when(yl == h)
                def _():
                    eg_sum[c] = tot

                @pl.when(yl != h)
                def _():
                    ysend[c] = tot.astype(BF16)

            rdma(ysend.at[c], yrecv.at[c], cy_s.at[c], cy_r.at[c], yp).start()
            return
        for way, first, later in ((0, rs_r0, rs_r), (1, rs_l0, rs_l)):
            tgt = z + 4 - step if way == 0 else z - 4 + step
            if step == 1:
                rs_move(c, 0, way, first.at[c], first.at[c]).wait_recv()
                add_into(c_rows(c, tgt, way), first.at[c])
            else:
                rs_move(c, step - 1, way, later.at[c, step - 2], later.at[c, step - 2]).wait_recv()
                add_into(c_rows(c, tgt), later.at[c, step - 2])
            rs_move(c, step, way, c_rows(c, tgt), later.at[c, step - 1]).start()

    def rs_drain(c):
        for way in (0, 1):
            rs_move(c, 0, way, rs_r0.at[c], rs_r0.at[c]).wait_send()
            for step in (1, 2, 3):
                rs_move(c, step, way, rs_r.at[c, 0], rs_r.at[c, 0]).wait_send()
        rdma(ysend.at[c], ysend.at[c], cy_s.at[c], cy_r.at[c], yp).wait_send()

    acc[...] = jnp.zeros_like(acc)
    zag(0)
    spread_wait(meta_in, meta_s, meta_r)
    spread_wait(hid_in, hid_s, hid_r)
    code_row = lax.broadcasted_iota(jnp.int32, (64, 128), 0).astype(F32)

    def place_rows(s, _):
        sel = (code_row == meta_in[s, 1:2, :]).astype(BF16)
        hid_rows[s] = dot(sel, hid_in[s], 0, 0).astype(BF16)
        return 0

    lax.fori_loop(0, ep_n, place_rows, 0)

    def back(c, lo, hi):
        def body(i, _):
            rows = pl.ds(i * 4, 4)
            res = dot(gat[c, rows].reshape(512, 512), w_perm[c], 1, 1)
            acc[rows] += res.reshape(4, 128, width_h)
            return 0

        lax.fori_loop(lo, hi, body, 0)

    def weight_part(c):
        def body(n, _):
            cols = pl.ds(pl.multiple_of(n * 256, 256), 256)
            left_rows = gat[c].reshape(ep_n * 128, 512)
            right_rows = hid_rows[:, :, cols].reshape(ep_n * 128, 256)
            part[c, :, cols] = dot(left_rows, right_rows, 0, 0).astype(BF16)
            return 0

        lax.fori_loop(0, width_h // 256, body, 0)

    def inside(c, f):
        pl.when((c >= 0) & (c < CHUNKS))(lambda: f(c))

    def sums(i):
        for step in (5, 4, 3, 2, 1):
            inside(i - 3 - step, lambda c: rs(c, step))

    def tick(i, _):
        inside(i + 1, ag0)
        inside(i, ag1)
        inside(i - 3, ag4)
        inside(i - 3, lambda c: back(c, 0, 2))
        inside(i - 1, ag2)
        inside(i - 3, lambda c: back(c, 2, 4))
        inside(i - 2, ag3)
        for step in range(1, 5):
            pl.when(i == 2 * step - 1)(lambda: zag(step))
        inside(i - 3, weight_part)
        inside(i - 3, lambda c: rs(c, 0))
        sums(i)
        return 0

    lax.fori_loop(0, CHUNKS + 3, tick, 0)

    def send_back(s, _):
        sel = (code_row == meta_in[s, 0:1, :]).astype(BF16)
        ret_send[s] = dot(sel, acc[s].astype(BF16), 1, 0).astype(BF16)
        return 0

    lax.fori_loop(0, ep_n, send_back, 0)
    spread_out(ret_send, ret_in, ret_s, ret_r)
    ret_in[me] = ret_send[me]
    build(0)

    def tail(i, _):
        sums(i)
        return 0

    lax.fori_loop(CHUNKS + 3, CHUNKS + 8, tail, 0)
    spread_wait(ret_in, ret_s, ret_r)

    def take(k):
        cols = slice(k * 128, (k + 1) * 128)
        sg_v[k] = dot(a_mat[:, cols], ret_in[...].reshape(1024, width_h), 0, 0).astype(BF16)

    outs = []
    for k in range(6):
        take(k)
        for m in (0, 1):
            cp = pltpu.make_async_copy(sg_v.at[k, pl.ds(m * 64, 64)], sg_out.at[m, k], loc.at[10 + 2 * k + m])
            cp.start()
            outs.append(cp)

    ag_drain(None)

    def drain(c, _):
        ag_drain(c)
        rs_drain(c)
        return 0

    lax.fori_loop(0, CHUNKS, drain, 0)
    spread_drain(meta_send, meta_s, meta_r)
    spread_drain(hid_send, hid_s, hid_r)
    spread_drain(ret_send, ret_s, ret_r)
    keep_own.wait()
    rdma(w_own, w_own, zy_s.at[0], zy_r.at[0], yp).wait_send()
    for way in (0, 1):
        for step in range(4):
            for yy in (0, 1):
                if step < 3 or yy == way:
                    rdma(w_own, w_own, z_s.at[way, step, yy], z_r.at[way, step, yy], yp).wait_send()
    for cp in outs:
        cp.wait()


def local(expert_ids, gates, hidden, cotangent, old_place, new_place, old_weights):
    micros, toks, tops = expert_ids.shape
    width_h, width_d = old_weights.shape[1:]
    lanes = micros * toks
    share = width_h // 16
    out_rows = width_d // 16
    ids_t = expert_ids.transpose(2, 0, 1).reshape(tops, lanes)
    gates_t = gates.transpose(2, 0, 1).reshape(tops, lanes)
    hid_t = hidden.transpose(0, 2, 1, 3)
    cot = cotangent.reshape(lanes, width_d)
    vmem, smem, hbm = (pl.BlockSpec(memory_space=m) for m in (pltpu.VMEM, pltpu.SMEM, pl.ANY))
    dma = pltpu.SemaphoreType.DMA
    v = pltpu.VMEM
    cw = width_d // CHUNKS
    scratch = [
        v((CHUNKS, 16, lanes, cw), BF16),
        v((16, share, width_d), BF16),
        v((width_h, width_d), BF16),
        v((CHUNKS, width_h, cw), BF16),
        v((lanes, width_d), BF16),
        v((tops, micros, toks, width_h), BF16),
        v((16 * micros * CAP, tops * lanes), BF16),
        v((16, micros * CAP, width_h), BF16),
        v((16, micros * CAP, width_h), BF16),
        v((16, lanes, width_h), BF16),
        v((16, lanes, width_h), F32),
        v((16, 8, lanes), F32),
        v((16, 8, lanes), F32),
        v((16, micros * CAP, width_h), BF16),
        v((16, micros * CAP, width_h), BF16),
        v((CHUNKS, cw, width_h), BF16),
        v((CHUNKS, 32, width_h), BF16),
        v((CHUNKS, 32, width_h), BF16),
        v((CHUNKS, 3, 64, width_h), BF16),
        v((CHUNKS, 3, 64, width_h), BF16),
        v((CHUNKS, 32, width_h), BF16),
        v((CHUNKS, 32, width_h), BF16),
        v((CHUNKS, 32, width_h), F32),
        v((share, width_d), BF16),
        v((tops, lanes, width_h), BF16),
        dma((22,)),
        dma((CHUNKS + 1, PIECES)),
        dma((CHUNKS + 1, PIECES)),
        dma((16,)), dma((16,)),
        dma((16,)), dma((16,)),
        dma((16,)), dma((16,)),
        dma((2, 4, 2)), dma((2, 4, 2)),
        dma((1,)), dma((1,)),
        dma((CHUNKS, 4, 2)), dma((CHUNKS, 4, 2)),
        dma((CHUNKS,)), dma((CHUNKS,)),
    ]
    slot_grads, new_weights, grads = pl.pallas_call(
        kernel,
        out_shape=(
            jax.ShapeDtypeStruct(hid_t.shape, BF16),
            jax.ShapeDtypeStruct((width_h, width_d), BF16),
            jax.ShapeDtypeStruct((out_rows, width_h), BF16),
        ),
        in_specs=[vmem, vmem, smem, smem, hbm, hbm, hbm],
        out_specs=(hbm, hbm, vmem),
        scratch_shapes=scratch,
        compiler_params=pltpu.CompilerParams(
            collective_id=0, has_side_effects=True, vmem_limit_bytes=60 * 1024 * 1024
        ),
    )(ids_t, gates_t, old_place, new_place, hid_t, cot, old_weights[0])
    return slot_grads.transpose(0, 2, 1, 3), new_weights[None], grads.T[None]


def solution(mesh):
    in_specs = (
        P(None, ("grp", "ep"), None),
        P(None, ("grp", "ep"), None),
        P(None, ("grp", "ep"), None, None),
        P(None, ("grp", "ep"), None),
        P(),
        P(),
        P("ep", None, None),
    )
    out_specs = (P(None, ("grp", "ep"), None, None), P("ep", None, None), P("ep", None, "grp"))
    return jax.shard_map(local, mesh=mesh, in_specs=in_specs, out_specs=out_specs, check_vma=False)
```

```python
import functools

import jax
import jax.numpy as jnp
from jax import lax
from jax.experimental import pallas as pl
from jax.experimental.pallas import tpu as pltpu
from jax.sharding import PartitionSpec as P

F32 = jnp.float32
BF16 = jnp.bfloat16
MESH = pl.DeviceIdType.MESH

CHUNKS = 5
PIECES = 10
CAP = 32
W_PARTS = ((0, 16), (16, 32))


def dot(a, b, ca, cb):
    return lax.dot_general(a, b, (((ca,), (cb,)), ((), ())), preferred_element_type=F32)


def kernel(
    ids, gates, old_place, new_place, hid, cot, w_old, ret_out, row_out, w_out, eg_out,
    gat, wsh_0, wsh_1, w_res, w_perm, cot_v, hid_v, a_mat, hid_send, hid_in, hid_rows, acc,
    meta_send, meta_in, ret_send, ret_in, part, rs_r0, rs_l0, rs_r, rs_l, ysend, yrecv, eg_sum,
    w_own, relay_y, relay_x,
    loc, ag_s, ag_r, hid_s, hid_r, meta_s, meta_r, ret_s, ret_r, z_s, z_r, zy_s, zy_r, c_s, c_r, cy_s, cy_r,
):
    g = lax.axis_index("grp")
    me = lax.axis_index("ep")
    z, yl = g // 2, g % 2
    core, xx, yh = me % 2, (me // 2) % 4, me // 8
    share = w_own.shape[0]
    ep_n = 16
    width_h = hid_v.shape[-1]

    def at_ep(dy=0, dx=0, dc=0):
        return (((yh + dy) % 2) * 4 + (xx + dx + 4) % 4) * 2 + (core + dc) % 2

    def to_ep(e):
        return (g, e)

    zp, zm = (((z + 1) % 8) * 2 + yl, me), (((z + 7) % 8) * 2 + yl, me)
    yp = (z * 2 + 1 - yl, me)
    left, right, yside, other = at_ep(dx=-1), at_ep(dx=1), at_ep(dy=1), at_ep(dc=1)

    def rdma(src, dst, ss, rs, dev):
        return pltpu.make_async_remote_copy(
            src_ref=src, dst_ref=dst, send_sem=ss, recv_sem=rs, device_id=dev, device_id_type=MESH
        )

    barrier = pltpu.get_barrier_semaphore()
    for d in range(1, ep_n):
        pl.semaphore_signal(barrier, 1, device_id=to_ep((me + d) % ep_n), device_id_type=MESH)
    for dev in (zp, zm, yp):
        pl.semaphore_signal(barrier, 1, device_id=dev, device_id_type=MESH)

    loads = [pltpu.make_async_copy(cot, cot_v, loc.at[0]), pltpu.make_async_copy(w_old, w_res, loc.at[1])]
    loads += [pltpu.make_async_copy(hid.at[:, k], hid_v.at[k], loc.at[2 + k]) for k in range(6)]

    def my_rows(w):
        lo, n = W_PARTS[w]
        return w_old.at[pl.ds(pl.multiple_of(g * share + lo, 16), n)]

    def by_core(e):
        return (e % 2) * 8 + e // 2

    def w_part(src, w):
        return (wsh_0, wsh_1)[w].at[src]

    mine = by_core(me)

    loads += [pltpu.make_async_copy(my_rows(w), w_part(mine, w), loc.at[8 + w]) for w in (0, 1)]
    for cp in loads:
        cp.start()
    pl.semaphore_wait(barrier, ep_n - 1 + 3)

    def block(job, src):
        if isinstance(job, str):
            return w_part(src, int(job))
        return gat.at[job, src]

    def half(job, src, h):
        if isinstance(job, str):
            cols = wsh_0.shape[2] // 2
            return (wsh_0, wsh_1)[int(job)].at[src, :, pl.ds(h * cols, cols)]
        return gat.at[job, src, pl.ds(h * 64, 64)]

    def number(job):
        if isinstance(job, str):
            return int(job)
        return job + 2

    def ag_send(job, piece, ref, dev, src=None):
        j = number(job)
        rdma(ref if src is None else src, ref, ag_s.at[j], ag_r.at[j, piece], to_ep(dev)).start()

    def ag_wait(job, piece, ref):
        j = number(job)
        rdma(ref, ref, ag_s.at[j], ag_r.at[j, piece], to_ep(other)).wait_recv()

    b_left, b_right, b_side = by_core(left), by_core(right), by_core(yside)
    b_x2 = by_core(at_ep(dx=2))
    b_yleft, b_yright, b_yx2 = by_core(at_ep(dy=1, dx=-1)), by_core(at_ep(dy=1, dx=1)), by_core(at_ep(dy=1, dx=2))
    plane, far_plane = core * 8 + yh * 4, core * 8 + (1 - yh) * 4
    o_plane, o_far_plane = (1 - core) * 8 + yh * 4, (1 - core) * 8 + (1 - yh) * 4

    def ag0(job):
        own = block(job, mine)
        src = my_rows(int(job)) if isinstance(job, str) else None
        ag_send(job, 0, own, right, src)
        ag_send(job, 1, own, left, src)
        ag_send(job, 2, own, yside, src)

    def ag1(job):
        ag_wait(job, 0, block(job, b_left))
        ag_send(job, 3, half(job, b_left, 0), right)
        ag_wait(job, 1, block(job, b_right))
        ag_send(job, 4, half(job, b_right, 1), left)
        ag_wait(job, 2, block(job, b_side))
        ag_send(job, 5, block(job, b_side), right)
        ag_send(job, 6, block(job, b_side), left)

    def ag2(job):
        ag_wait(job, 3, half(job, b_x2, 0))
        ag_wait(job, 4, half(job, b_x2, 1))
        ag_send(job, 7, block(job, b_x2), yside)
        if isinstance(job, str):
            loads[8 + int(job)].wait()
        ag_send(job, 8, block(job, pl.ds(plane, 4)), other)

    def ag3(job):
        ag_wait(job, 5, block(job, b_yleft))
        ag_wait(job, 6, block(job, b_yright))
        ag_wait(job, 7, block(job, b_yx2))
        ag_send(job, 9, block(job, pl.ds(far_plane, 4)), other)

    def ag4(job):
        ag_wait(job, 8, block(job, pl.ds(o_plane, 4)))
        ag_wait(job, 9, block(job, pl.ds(o_far_plane, 4)))

    def ag_drain(job):
        ref = block(job, pl.ds(0, 15))
        rdma(ref, ref, ag_s.at[number(job)], ag_r.at[number(job), 0], to_ep(other)).wait_send()

    ag0("0")
    ag0("1")

    def chooser(c):
        i = lax.broadcasted_iota(jnp.int32, (640, 128), 0)
        j = lax.broadcasted_iota(jnp.int32, (640, 128), 1)
        return (i == (j // 32) * 160 + c * 32 + j % 32).astype(BF16)

    loads[0].wait()

    def perm_cot(c, _):
        sel = chooser(c)
        for q in range(4):
            gat[c, mine, :, q * 128 : (q + 1) * 128] = dot(
                cot_v[:, q * 640 : (q + 1) * 640], sel, 1, 0
            ).astype(BF16)
        return 0

    lax.fori_loop(0, CHUNKS, perm_cot, 0)

    ag1("0")

    lane = lax.broadcasted_iota(jnp.int32, (16, 128), 1)
    row16 = lax.broadcasted_iota(jnp.int32, (16, 128), 0)
    micro = (lane[:1] >= 64).astype(F32)
    ui = lax.broadcasted_iota(jnp.int32, (128, 128), 0)
    uj = lax.broadcasted_iota(jnp.int32, (128, 128), 1)
    upper = ((ui < uj) & ((ui >= 64) == (uj >= 64))).astype(BF16)

    def lanes_of(ref, k):
        both = ref[k]
        return jnp.concatenate([both[0:1], both[1:2]], axis=1)

    slot_of = [jnp.zeros((16, 128), F32), jnp.zeros((16, 128), F32)]
    source = jnp.int32(0)
    for e in range(16):
        slot_of[0] = jnp.where(row16 == e, old_place[e].astype(F32), slot_of[0])
        slot_of[1] = jnp.where(row16 == e, new_place[e].astype(F32), slot_of[1])
        source = source + jnp.where(new_place[e] == me, old_place[e], 0)
    target = [[], []]
    for which in (0, 1):
        slots, hits = [], []
        for k in range(6):
            eq = lanes_of(ids, k) == row16
            slot = jnp.sum(jnp.where(eq, slot_of[which], 0.0), axis=0, keepdims=True)
            slots.append(slot)
            hits.append(row16.astype(F32) == slot)
        routed = sum(h.astype(F32) for h in hits)
        rank = dot(routed.astype(BF16), upper, 1, 0)
        for k in range(6):
            nth = jnp.sum(jnp.where(hits[k], rank, 0.0), axis=0, keepdims=True)
            target[which].append(slots[k] * (2 * CAP) + micro * CAP + nth)
        coded = jnp.where(routed > 0.5, rank + micro * CAP, -1.0)
        for s in range(16):
            meta_send[s, which : which + 1, :] = coded[s : s + 1, :]

    for k in range(6):
        row_out[k : k + 1, :] = target[0][k]

    def build(which):
        rows = lax.broadcasted_iota(jnp.int32, (1024, 128), 0).astype(F32)
        for k in range(6):
            a_mat[:, k * 128 : (k + 1) * 128] = jnp.where(
                rows == target[which][k], lanes_of(gates, k), 0.0
            ).astype(BF16)

    def spread_out(src, dst, ss, rs, ways=range(1, 16)):
        for d in ways:
            e = (me + d) % ep_n
            rdma(src.at[e], dst.at[me], ss.at[0], rs.at[0], to_ep(e)).start()

    def spread_wait(dst, ss, rs):
        ref = dst.at[pl.ds(0, ep_n - 1)]
        rdma(ref, ref, ss.at[0], rs.at[0], to_ep(other)).wait_recv()

    def spread_drain(src, ss, rs):
        ref = src.at[pl.ds(0, ep_n - 1)]
        rdma(ref, ref, ss.at[0], rs.at[0], to_ep(other)).wait_send()

    here, near, far = me % 8, yh * 8, (1 - yh) * 8
    side = far + here
    upper_rows, lower_rows = pl.ds(0, CAP), pl.ds(CAP, CAP)

    def swap(which, src, dst, piece, dev):
        ss, rs = (hid_s, hid_r) if which == 0 else (ret_s, ret_r)
        return rdma(src, dst, ss.at[0], rs.at[piece], to_ep(dev))

    def swap_far(which, send):
        ya, xb = relay_y.at[which], relay_x.at[which]
        for d in range(1, 8):
            t = (here + d) % 8
            swap(which, send.at[far + t, lower_rows], xb.at[here], 0, near + t).start()
        swap(which, send.at[pl.ds(far, 8), upper_rows], ya, 1, side).start()
        relay_x[which, here] = send[side, lower_rows]

    def swap_near(which, send, into):
        for d in range(1, 8):
            t = (here + d) % 8
            swap(which, send.at[near + t], into.at[me], 2, near + t).start()
        into[me] = send[me]

    def swap_pass(which, into):
        ya, xb = relay_y.at[which], relay_x.at[which]
        swap(which, xb.at[pl.ds(0, 7)], xb.at[pl.ds(0, 7)], 0, side).wait_recv()
        swap(which, xb, into.at[pl.ds(near, 8), lower_rows], 3, side).start()
        swap(which, ya, ya, 1, side).wait_recv()
        for d in range(1, 8):
            t = (here + d) % 8
            swap(which, ya.at[t], into.at[side, upper_rows], 4, near + t).start()
        into[side, upper_rows] = relay_y[which, here]

    def swap_wait(which, into):
        seven = pl.ds(0, 7)
        swap(which, into.at[seven], into.at[seven], 2, side).wait_recv()
        ref = into.at[pl.ds(far, 8), lower_rows]
        swap(which, ref, ref, 3, side).wait_recv()
        ref = into.at[seven, upper_rows]
        swap(which, ref, ref, 4, side).wait_recv()

    def swap_drain(which):
        ref = hid_rows.at[pl.ds(0, 11)]
        swap(which, ref, ref, 0, side).wait_send()

    spread_out(meta_send, meta_in, meta_s, meta_r)
    meta_in[me] = meta_send[me]
    ag1("1")
    ag2("0")
    ag0(0)
    build(1)
    for cp in loads[2:8]:
        cp.wait()
    def pack(i, _):
        rows = pl.ds(pl.multiple_of(i * 256, 256), 256)
        res = dot(a_mat[rows, :], hid_v[...].reshape(6 * 128, width_h), 1, 0).astype(BF16)
        hid_send[pl.ds(i * 4, 4)] = res.reshape(4, 64, width_h)
        return 0

    lax.fori_loop(0, 4, pack, 0)

    ag3("0")
    ag2("1")


    def w_rows(w, zz, yy):
        lo, n = W_PARTS[w]
        return w_out.at[(zz + 16) % 8, yy, pl.ds(lo, n)]

    def w_pair(w, zz):
        lo, n = W_PARTS[w]
        return w_out.at[(zz + 16) % 8, :, pl.ds(lo, n)]

    def own_part(w):
        lo, n = W_PARTS[w]
        return w_own.at[pl.ds(lo, n)]

    def z_copy(w, src, dst, way, step, yy):
        return rdma(src, dst, z_s.at[w], z_r.at[w, way, step, yy], zp if way == 0 else zm)

    def keep_own(w):
        return pltpu.make_async_copy(own_part(w), w_rows(w, z, yl), loc.at[10 + w])

    def z_begin(w):
        lo, n = W_PARTS[w]
        ag4(str(w))
        w_own[lo : lo + n] = (wsh_0, wsh_1)[w][by_core(source)]
        rdma(own_part(w), w_rows(w, z, yl), zy_s.at[w], zy_r.at[w], yp).start()
        for way in (0, 1):
            z_copy(w, own_part(w), w_rows(w, z, yl), way, 0, yl).start()
        keep_own(w).start()

    def zag(w, step):
        if step == 0:
            ref = w_rows(w, z, 1 - yl)
            rdma(ref, ref, zy_s.at[w], zy_r.at[w], yp).wait_recv()
            for way in (0, 1):
                z_copy(w, ref, ref, way, 0, 1 - yl).start()
            return
        for way in (0, 1):
            zz = z - step if way == 0 else z + step
            if step == 1:
                for yy in (0, 1):
                    ref = w_rows(w, zz, yy)
                    z_copy(w, ref, ref, way, 0, yy).wait_recv()
            else:
                ref = w_pair(w, zz) if step < 4 else w_rows(w, zz, way)
                z_copy(w, ref, ref, way, step - 1, 0).wait_recv()
            if step < 4:
                ref = w_pair(w, zz) if step < 3 else w_rows(w, zz, way)
                z_copy(w, ref, ref, way, step, 0).start()

    z_begin(0)
    ag1(0)
    ag0(1)
    swap_far(0, hid_send)
    zag(0, 0)
    loads[1].wait()

    def perm_w(c, _):
        sel = chooser(c)
        for q in range(4):
            w_perm[c, :, q * 128 : (q + 1) * 128] = dot(
                w_res[:, q * 640 : (q + 1) * 640], sel, 1, 0
            ).astype(BF16)
        return 0

    ag3("1")
    lax.fori_loop(0, 2, perm_w, 0)
    ag2(0)
    z_begin(1)
    ag1(1)
    swap_near(0, hid_send, hid_in)
    lax.fori_loop(2, CHUNKS, perm_w, 0)
    ag3(0)
    zag(0, 1)
    zag(1, 0)
    acc[...] = jnp.zeros_like(acc)
    ag2(1)
    swap_pass(0, hid_in)
    ag0(2)

    def c_rows(c, zz, h=None):
        start = pl.multiple_of(((zz + 16) % 8) * 64 + (0 if h is None else h * 32), 32)
        return part.at[c, pl.ds(start, 64 if h is None else 32)]

    def add_into(ref, other_ref):
        ref[...] = (ref[...].astype(F32) + other_ref[...].astype(F32)).astype(BF16)

    def rs_move(c, step, way, src, dst):
        return rdma(src, dst, c_s.at[c], c_r.at[c, step, way], zp if way == 0 else zm)

    def rs(c, step):
        if step == 0:
            rs_move(c, 0, 0, c_rows(c, z + 4, 0), rs_r0.at[c]).start()
            rs_move(c, 0, 1, c_rows(c, z - 4, 1), rs_l0.at[c]).start()
            return
        if step == 5:
            rdma(yrecv.at[c], yrecv.at[c], cy_s.at[c], cy_r.at[c], yp).wait_recv()
            tot = eg_sum[c] + yrecv[c].astype(F32)
            eg_out[pl.ds(pl.multiple_of(c * 32, 32), 32), :] = (tot / 16.0).astype(BF16)
            return
        if step == 4:
            rs_move(c, 3, 0, rs_r.at[c, 2], rs_r.at[c, 2]).wait_recv()
            rs_move(c, 3, 1, rs_l.at[c, 2], rs_l.at[c, 2]).wait_recv()
            for h in (0, 1):
                rows = pl.ds(h * 32, 32)
                tot = (
                    c_rows(c, z, h)[...].astype(F32)
                    + rs_r[c, 2, rows, :].astype(F32)
                    + rs_l[c, 2, rows, :].astype(F32)
                )

                @pl.when(yl == h)
                def _():
                    eg_sum[c] = tot

                @pl.when(yl != h)
                def _():
                    ysend[c] = tot.astype(BF16)

            rdma(ysend.at[c], yrecv.at[c], cy_s.at[c], cy_r.at[c], yp).start()
            return
        for way, first, later in ((0, rs_r0, rs_r), (1, rs_l0, rs_l)):
            tgt = z + 4 - step if way == 0 else z - 4 + step
            if step == 1:
                rs_move(c, 0, way, first.at[c], first.at[c]).wait_recv()
                add_into(c_rows(c, tgt, way), first.at[c])
            else:
                rs_move(c, step - 1, way, later.at[c, step - 2], later.at[c, step - 2]).wait_recv()
                add_into(c_rows(c, tgt), later.at[c, step - 2])
            rs_move(c, step, way, c_rows(c, tgt), later.at[c, step - 1]).start()

    def rs_drain(c):
        ref = part.at[c, pl.ds(0, 2 * (32 + 3 * 64))]
        rdma(ref, ref, c_s.at[c], c_r.at[c, 0, 0], zp).wait_send()
        rdma(ysend.at[c], ysend.at[c], cy_s.at[c], cy_r.at[c], yp).wait_send()

    code_row = lax.broadcasted_iota(jnp.int32, (64, 128), 0).astype(F32)

    def place_rows(s, _):
        sel = (code_row == meta_in[s, 1:2, :]).astype(BF16)
        hid_rows[by_core(s)] = dot(sel, hid_in[s], 0, 0).astype(BF16)
        return 0


    def back(c):
        def body(i, _):
            rows = pl.ds(i * 4, 4)
            res = dot(gat[c, rows].reshape(512, 512), w_perm[c], 1, 1)
            acc[rows] += res.reshape(4, 128, width_h)
            return 0

        lax.fori_loop(0, 4, body, 0)

    def pack_back(first):
        def body(t, _):
            e = first + t
            sel = (code_row == meta_in[e, 0:1, :]).astype(BF16)
            ret_send[e] = dot(sel, acc[by_core(e)].astype(BF16), 1, 0).astype(BF16)
            return 0

        lax.fori_loop(0, 8, body, 0)

    def weight_part(c):
        def body(n, _):
            rows = pl.ds(pl.multiple_of(n * 256, 256), 256)
            left_rows = gat[c, :, :, rows].reshape(ep_n * 128, 256)
            part[c, rows] = dot(left_rows, hid_rows[...].reshape(ep_n * 128, width_h), 0, 0).astype(BF16)
            return 0

        lax.fori_loop(0, 2, body, 0)

    def inside(c, f):
        pl.when((c >= 0) & (c < CHUNKS))(lambda: f(c))

    def sums(i):
        for step in (5, 4, 3, 2, 1):
            inside(i - step, lambda c: rs(c, step))

    ag4(0)
    back(0)
    zag(0, 2)
    ag3(1)
    ag1(2)
    zag(1, 1)
    ag4(1)
    back(1)
    zag(0, 3)
    ag0(3)
    ag2(2)
    spread_wait(meta_in, meta_s, meta_r)
    swap_wait(0, hid_in)
    lax.fori_loop(0, ep_n, place_rows, 0)
    weight_part(0)
    rs(0, 0)
    ag3(2)
    ag1(3)
    ag0(4)
    zag(1, 2)
    weight_part(1)
    rs(1, 0)
    rs(0, 1)

    def tick(i, _):
        inside(i + 1, ag2)
        inside(i + 2, ag1)
        ag4(i)
        back(i)
        sums(i)
        weight_part(i)
        rs(i, 0)
        inside(i + 1, ag3)
        pl.when(i == 2)(lambda: zag(1, 3))
        return 0

    lax.fori_loop(2, CHUNKS, tick, 0)
    pack_back(far)
    swap_far(1, ret_send)
    pack_back(near)
    swap_near(1, ret_send, ret_in)

    def tail(i, _):
        sums(i)
        return 0

    lax.fori_loop(CHUNKS, CHUNKS + 2, tail, 0)
    swap_pass(1, ret_in)
    lax.fori_loop(CHUNKS + 2, CHUNKS + 5, tail, 0)
    swap_wait(1, ret_in)
    keep_ret = pltpu.make_async_copy(ret_in, ret_out, loc.at[12])
    keep_ret.start()
    zag(0, 4)
    zag(1, 4)

    ag_drain("0")
    ag_drain("1")

    def drain(c, _):
        ag_drain(c)
        rs_drain(c)
        return 0

    lax.fori_loop(0, CHUNKS, drain, 0)
    spread_drain(meta_send, meta_s, meta_r)
    swap_drain(0)
    swap_drain(1)
    for w in (0, 1):
        keep_own(w).wait()
        rdma(own_part(w), own_part(w), zy_s.at[w], zy_r.at[w], yp).wait_send()
        lo, n = W_PARTS[w]
        sent = w_out.at[pl.ds(0, 7), :, pl.ds(lo, n)]
        z_copy(w, sent, sent, 0, 0, 0).wait_send()
    keep_ret.wait()


def finish(ret_h, rows_at, gates, w_in, eg_in, sg_out, w_out, eg_out, ret, w_v, sems):
    load = pltpu.make_async_copy(ret_h, ret, sems.at[sems.shape[0] - 1])
    load.start()
    pieces = (sems.shape[0] - 1) // 2
    n = w_in.shape[0] // pieces
    rows_of = [pl.ds(p * n, n) for p in range(pieces)]
    ups = [pltpu.make_async_copy(w_in.at[r], w_v.at[r], sems.at[p]) for p, r in enumerate(rows_of)]
    downs = [pltpu.make_async_copy(w_v.at[r], w_out.at[r], sems.at[pieces + p]) for p, r in enumerate(rows_of)]
    for cp in ups:
        cp.start()
    eg_out[...] = eg_in[...]
    load.wait()
    rows = lax.broadcasted_iota(jnp.int32, (1024, 128), 0).astype(F32)
    for k in range(6):
        for p in range(k * pieces // 6, (k + 1) * pieces // 6):
            ups[p].wait()
            downs[p].start()
        both = gates[k]
        gate = jnp.concatenate([both[0:1], both[1:2]], axis=1)
        sel = jnp.where(rows == rows_at[k : k + 1, :], gate, 0.0).astype(BF16)
        got = dot(sel, ret[...].reshape(1024, ret.shape[-1]), 0, 0).astype(BF16)
        sg_out[0, k] = got[:64]
        sg_out[1, k] = got[64:]
    for cp in downs:
        cp.wait()


def local(expert_ids, gates, hidden, cotangent, old_place, new_place, old_weights):
    micros, toks, tops = expert_ids.shape
    width_h, width_d = old_weights.shape[1:]
    lanes = micros * toks
    share = width_h // 16
    out_rows = width_d // 16
    ids_t = expert_ids.transpose(2, 0, 1)
    gates_t = gates.transpose(2, 0, 1)
    hid_t = hidden.transpose(0, 2, 1, 3)
    cot = cotangent.reshape(lanes, width_d)
    vmem, smem, hbm = (pl.BlockSpec(memory_space=m) for m in (pltpu.VMEM, pltpu.SMEM, pl.ANY))
    dma = pltpu.SemaphoreType.DMA
    v = pltpu.VMEM
    cw = width_d // CHUNKS
    scratch = [
        v((CHUNKS, 16, lanes, cw), BF16),
        v((16, W_PARTS[0][1], width_d), BF16),
        v((16, W_PARTS[1][1], width_d), BF16),
        v((width_h, width_d), BF16),
        v((CHUNKS, width_h, cw), BF16),
        v((lanes, width_d), BF16),
        v((tops, micros, toks, width_h), BF16),
        v((16 * micros * CAP, tops * lanes), BF16),
        v((16, micros * CAP, width_h), BF16),
        v((16, micros * CAP, width_h), BF16),
        v((16, lanes, width_h), BF16),
        v((16, lanes, width_h), F32),
        v((16, 8, lanes), F32),
        v((16, 8, lanes), F32),
        v((16, micros * CAP, width_h), BF16),
        v((16, micros * CAP, width_h), BF16),
        v((CHUNKS, cw, width_h), BF16),
        v((CHUNKS, 32, width_h), BF16),
        v((CHUNKS, 32, width_h), BF16),
        v((CHUNKS, 3, 64, width_h), BF16),
        v((CHUNKS, 3, 64, width_h), BF16),
        v((CHUNKS, 32, width_h), BF16),
        v((CHUNKS, 32, width_h), BF16),
        v((CHUNKS, 32, width_h), F32),
        v((share, width_d), BF16),
        v((2, 8, CAP, width_h), BF16),
        v((2, 8, CAP, width_h), BF16),
        dma((13,)),
        dma((CHUNKS + 2,)),
        dma((CHUNKS + 2, PIECES)),
        dma((1,)), dma((5,)),
        dma((1,)), dma((1,)),
        dma((1,)), dma((5,)),
        dma((2,)), dma((2, 2, 4, 2)),
        dma((2,)), dma((2,)),
        dma((CHUNKS,)), dma((CHUNKS, 4, 2)),
        dma((CHUNKS,)), dma((CHUNKS,)),
    ]
    ret, rows_at, weights, grads = pl.pallas_call(
        kernel,
        out_shape=(
            jax.ShapeDtypeStruct((16, micros * CAP, width_h), BF16),
            jax.ShapeDtypeStruct((8, lanes), F32),
            jax.ShapeDtypeStruct((8, 2, share, width_d), BF16),
            jax.ShapeDtypeStruct((out_rows, width_h), BF16),
        ),
        in_specs=[vmem, vmem, smem, smem, hbm, hbm, hbm],
        out_specs=(hbm, vmem, hbm, vmem),
        scratch_shapes=scratch,
        compiler_params=pltpu.CompilerParams(
            collective_id=0, has_side_effects=True, vmem_limit_bytes=60 * 1024 * 1024
        ),
    )(ids_t, gates_t, old_place, new_place, hid_t, cot, old_weights[0])
    weights = weights.reshape(width_h, width_d)
    slot_grads, new_weights, grads = pl.pallas_call(
        finish,
        out_shape=(
            jax.ShapeDtypeStruct(hid_t.shape, BF16),
            jax.ShapeDtypeStruct(weights.shape, BF16),
            jax.ShapeDtypeStruct(grads.shape, BF16),
        ),
        in_specs=[hbm, vmem, vmem, hbm, vmem],
        out_specs=(vmem, hbm, vmem),
        scratch_shapes=[v(ret.shape, BF16), v(weights.shape, BF16), dma((25,))],
        compiler_params=pltpu.CompilerParams(vmem_limit_bytes=60 * 1024 * 1024),
    )(ret, rows_at, gates_t, weights, grads)
    return slot_grads.transpose(0, 2, 1, 3), new_weights[None], grads.T[None]


def solution(mesh):
    in_specs = (
        P(None, ("grp", "ep"), None),
        P(None, ("grp", "ep"), None),
        P(None, ("grp", "ep"), None, None),
        P(None, ("grp", "ep"), None),
        P(),
        P(),
        P("ep", None, None),
    )
    out_specs = (P(None, ("grp", "ep"), None, None), P("ep", None, None), P("ep", None, "grp"))
    return jax.shard_map(local, mesh=mesh, in_specs=in_specs, out_specs=out_specs, check_vma=False)
```

```python
import functools

import jax
import jax.numpy as jnp
from jax import lax
from jax.experimental import pallas as pl
from jax.experimental.pallas import tpu as pltpu
from jax.sharding import PartitionSpec as P

F32 = jnp.float32
BF16 = jnp.bfloat16
MESH = pl.DeviceIdType.MESH

CHUNKS = 5
PIECES = 10
CAP = 32
W_PARTS = ((0, 16), (16, 32))


def dot(a, b, ca, cb):
    return lax.dot_general(a, b, (((ca,), (cb,)), ((), ())), preferred_element_type=F32)


def kernel(
    ids, gates, old_place, new_place, hid, cot, w_old, ret_out, row_out, w_out, eg_out,
    gat, wsh_0, wsh_1, w_res, w_perm, cot_v, hid_v, a_mat, hid_send, hid_in, hid_rows, acc,
    meta_send, meta_in, ret_send, ret_in, part, rs_r0, rs_l0, rs_r, rs_l, ysend, yrecv, eg_sum,
    w_own, relay_y, relay_x,
    loc, ag_s, ag_r, hid_s, hid_r, meta_s, meta_r, ret_s, ret_r, z_s, z_r, zy_s, zy_r, c_s, c_r, cy_s, cy_r,
):
    g = lax.axis_index("grp")
    me = lax.axis_index("ep")
    z, yl = g // 2, g % 2
    core, xx, yh = me % 2, (me // 2) % 4, me // 8
    share = w_own.shape[0]
    ep_n = 16
    width_h = hid_v.shape[-1]

    def at_ep(dy=0, dx=0, dc=0):
        return (((yh + dy) % 2) * 4 + (xx + dx + 4) % 4) * 2 + (core + dc) % 2

    def to_ep(e):
        return (g, e)

    zp, zm = (((z + 1) % 8) * 2 + yl, me), (((z + 7) % 8) * 2 + yl, me)
    yp = (z * 2 + 1 - yl, me)
    left, right, yside, other = at_ep(dx=-1), at_ep(dx=1), at_ep(dy=1), at_ep(dc=1)

    def rdma(src, dst, ss, rs, dev):
        return pltpu.make_async_remote_copy(
            src_ref=src, dst_ref=dst, send_sem=ss, recv_sem=rs, device_id=dev, device_id_type=MESH
        )

    barrier = pltpu.get_barrier_semaphore()
    for d in range(1, ep_n):
        pl.semaphore_signal(barrier, 1, device_id=to_ep((me + d) % ep_n), device_id_type=MESH)
    for dev in (zp, zm, yp):
        pl.semaphore_signal(barrier, 1, device_id=dev, device_id_type=MESH)

    loads = [pltpu.make_async_copy(cot, cot_v, loc.at[0]), pltpu.make_async_copy(w_old, w_res, loc.at[1])]
    loads += [pltpu.make_async_copy(hid.at[:, k], hid_v.at[k], loc.at[2 + k]) for k in range(6)]

    def my_rows(w):
        lo, n = W_PARTS[w]
        return w_old.at[pl.ds(pl.multiple_of(g * share + lo, 16), n)]

    def by_core(e):
        return (e % 2) * 8 + e // 2

    def w_part(src, w):
        return (wsh_0, wsh_1)[w].at[src]

    mine = by_core(me)

    loads += [pltpu.make_async_copy(my_rows(w), w_part(mine, w), loc.at[8 + w]) for w in (0, 1)]
    for cp in loads:
        cp.start()
    pl.semaphore_wait(barrier, ep_n - 1 + 3)

    def block(job, src):
        if isinstance(job, str):
            return w_part(src, int(job))
        return gat.at[job, src]

    def half(job, src, h):
        if isinstance(job, str):
            cols = wsh_0.shape[2] // 2
            return (wsh_0, wsh_1)[int(job)].at[src, :, pl.ds(h * cols, cols)]
        return gat.at[job, src, pl.ds(h * 64, 64)]

    def number(job):
        if isinstance(job, str):
            return int(job)
        return job + 2

    def ag_send(job, piece, ref, dev, src=None):
        j = number(job)
        rdma(ref if src is None else src, ref, ag_s.at[j], ag_r.at[j, piece], to_ep(dev)).start()

    def ag_wait(job, piece, ref):
        j = number(job)
        rdma(ref, ref, ag_s.at[j], ag_r.at[j, piece], to_ep(other)).wait_recv()

    b_left, b_right, b_side = by_core(left), by_core(right), by_core(yside)
    b_x2 = by_core(at_ep(dx=2))
    b_yleft, b_yright, b_yx2 = by_core(at_ep(dy=1, dx=-1)), by_core(at_ep(dy=1, dx=1)), by_core(at_ep(dy=1, dx=2))
    plane, far_plane = core * 8 + yh * 4, core * 8 + (1 - yh) * 4
    o_plane, o_far_plane = (1 - core) * 8 + yh * 4, (1 - core) * 8 + (1 - yh) * 4

    def ag0(job):
        own = block(job, mine)
        src = my_rows(int(job)) if isinstance(job, str) else None
        ag_send(job, 0, own, right, src)
        ag_send(job, 1, own, left, src)
        ag_send(job, 2, own, yside, src)

    def ag1(job):
        ag_wait(job, 0, block(job, b_left))
        ag_send(job, 3, half(job, b_left, 0), right)
        ag_wait(job, 1, block(job, b_right))
        ag_send(job, 4, half(job, b_right, 1), left)
        ag_wait(job, 2, block(job, b_side))
        ag_send(job, 5, block(job, b_side), right)
        ag_send(job, 6, block(job, b_side), left)

    def ag2(job):
        ag_wait(job, 3, half(job, b_x2, 0))
        ag_wait(job, 4, half(job, b_x2, 1))
        ag_send(job, 7, block(job, b_x2), yside)
        if isinstance(job, str):
            loads[8 + int(job)].wait()
        ag_send(job, 8, block(job, pl.ds(plane, 4)), other)

    def ag3(job):
        ag_wait(job, 5, block(job, b_yleft))
        ag_wait(job, 6, block(job, b_yright))
        ag_wait(job, 7, block(job, b_yx2))
        ag_send(job, 9, block(job, pl.ds(far_plane, 4)), other)

    def ag4(job):
        ag_wait(job, 8, block(job, pl.ds(o_plane, 4)))
        ag_wait(job, 9, block(job, pl.ds(o_far_plane, 4)))

    def ag_drain(job):
        ref = block(job, pl.ds(0, 15))
        rdma(ref, ref, ag_s.at[number(job)], ag_r.at[number(job), 0], to_ep(other)).wait_send()

    ag0("0")
    ag0("1")

    def chooser(c):
        i = lax.broadcasted_iota(jnp.int32, (640, 128), 0)
        j = lax.broadcasted_iota(jnp.int32, (640, 128), 1)
        return (i == (j // 32) * 160 + c * 32 + j % 32).astype(BF16)

    loads[0].wait()

    def perm_cot(c, _):
        sel = chooser(c)
        for q in range(4):
            gat[c, mine, :, q * 128 : (q + 1) * 128] = dot(
                cot_v[:, q * 640 : (q + 1) * 640], sel, 1, 0
            ).astype(BF16)
        return 0

    lax.fori_loop(0, CHUNKS, perm_cot, 0)

    ag1("0")
    ag1("1")
    ag0(0)
    ag2("0")

    lane = lax.broadcasted_iota(jnp.int32, (16, 128), 1)
    row16 = lax.broadcasted_iota(jnp.int32, (16, 128), 0)
    micro = (lane[:1] >= 64).astype(F32)
    ui = lax.broadcasted_iota(jnp.int32, (128, 128), 0)
    uj = lax.broadcasted_iota(jnp.int32, (128, 128), 1)
    upper = ((ui < uj) & ((ui >= 64) == (uj >= 64))).astype(BF16)

    def lanes_of(ref, k):
        both = ref[k]
        return jnp.concatenate([both[0:1], both[1:2]], axis=1)

    slot_of = [jnp.zeros((16, 128), F32), jnp.zeros((16, 128), F32)]
    source = jnp.int32(0)
    for e in range(16):
        slot_of[0] = jnp.where(row16 == e, old_place[e].astype(F32), slot_of[0])
        slot_of[1] = jnp.where(row16 == e, new_place[e].astype(F32), slot_of[1])
        source = source + jnp.where(new_place[e] == me, old_place[e], 0)
    target = [[], []]
    for which in (0, 1):
        slots, hits = [], []
        for k in range(6):
            eq = lanes_of(ids, k) == row16
            slot = jnp.sum(jnp.where(eq, slot_of[which], 0.0), axis=0, keepdims=True)
            slots.append(slot)
            hits.append(row16.astype(F32) == slot)
        routed = sum(h.astype(F32) for h in hits)
        rank = dot(routed.astype(BF16), upper, 1, 0)
        for k in range(6):
            nth = jnp.sum(jnp.where(hits[k], rank, 0.0), axis=0, keepdims=True)
            target[which].append(slots[k] * (2 * CAP) + micro * CAP + nth)
        coded = jnp.where(routed > 0.5, rank + micro * CAP, -1.0)
        for s in range(16):
            meta_send[s, which : which + 1, :] = coded[s : s + 1, :]

    for k in range(6):
        row_out[k : k + 1, :] = target[0][k]

    def build(which):
        rows = lax.broadcasted_iota(jnp.int32, (1024, 128), 0).astype(F32)
        for k in range(6):
            a_mat[:, k * 128 : (k + 1) * 128] = jnp.where(
                rows == target[which][k], lanes_of(gates, k), 0.0
            ).astype(BF16)

    def spread_out(src, dst, ss, rs, ways=range(1, 16)):
        for d in ways:
            e = (me + d) % ep_n
            rdma(src.at[e], dst.at[me], ss.at[0], rs.at[0], to_ep(e)).start()

    def spread_wait(dst, ss, rs):
        ref = dst.at[pl.ds(0, ep_n - 1)]
        rdma(ref, ref, ss.at[0], rs.at[0], to_ep(other)).wait_recv()

    def spread_drain(src, ss, rs):
        ref = src.at[pl.ds(0, ep_n - 1)]
        rdma(ref, ref, ss.at[0], rs.at[0], to_ep(other)).wait_send()

    here, near, far = me % 8, yh * 8, (1 - yh) * 8
    side = far + here
    upper_rows, lower_rows = pl.ds(0, CAP), pl.ds(CAP, CAP)

    def swap(which, src, dst, piece, dev):
        ss, rs = (hid_s, hid_r) if which == 0 else (ret_s, ret_r)
        return rdma(src, dst, ss.at[0], rs.at[piece], to_ep(dev))

    def swap_far(which, send):
        ya, xb = relay_y.at[which], relay_x.at[which]
        for d in range(1, 8):
            t = (here + d) % 8
            swap(which, send.at[far + t, lower_rows], xb.at[here], 0, near + t).start()
        swap(which, send.at[pl.ds(far, 8), upper_rows], ya, 1, side).start()
        relay_x[which, here] = send[side, lower_rows]

    def swap_near(which, send, into):
        for d in range(1, 8):
            t = (here + d) % 8
            swap(which, send.at[near + t], into.at[me], 2, near + t).start()
        into[me] = send[me]

    def swap_pass(which, into):
        ya, xb = relay_y.at[which], relay_x.at[which]
        swap(which, xb.at[pl.ds(0, 7)], xb.at[pl.ds(0, 7)], 0, side).wait_recv()
        swap(which, xb, into.at[pl.ds(near, 8), lower_rows], 3, side).start()
        swap(which, ya, ya, 1, side).wait_recv()
        for d in range(1, 8):
            t = (here + d) % 8
            swap(which, ya.at[t], into.at[side, upper_rows], 4, near + t).start()
        into[side, upper_rows] = relay_y[which, here]

    def swap_wait(which, into):
        seven = pl.ds(0, 7)
        swap(which, into.at[seven], into.at[seven], 2, side).wait_recv()
        ref = into.at[pl.ds(far, 8), lower_rows]
        swap(which, ref, ref, 3, side).wait_recv()
        ref = into.at[seven, upper_rows]
        swap(which, ref, ref, 4, side).wait_recv()

    def swap_drain(which):
        ref = hid_rows.at[pl.ds(0, 11)]
        swap(which, ref, ref, 0, side).wait_send()

    spread_out(meta_send, meta_in, meta_s, meta_r)
    meta_in[me] = meta_send[me]
    build(1)
    for cp in loads[2:8]:
        cp.wait()
    def pack(i, _):
        rows = pl.ds(pl.multiple_of(i * 256, 256), 256)
        res = dot(a_mat[rows, :], hid_v[...].reshape(6 * 128, width_h), 1, 0).astype(BF16)
        hid_send[pl.ds(i * 4, 4)] = res.reshape(4, 64, width_h)
        return 0

    lax.fori_loop(0, 4, pack, 0)

    ag3("0")
    ag2("1")


    def w_rows(w, zz, yy):
        lo, n = W_PARTS[w]
        return w_out.at[(zz + 16) % 8, yy, pl.ds(lo, n)]

    def w_pair(w, zz):
        lo, n = W_PARTS[w]
        return w_out.at[(zz + 16) % 8, :, pl.ds(lo, n)]

    def own_part(w):
        lo, n = W_PARTS[w]
        return w_own.at[pl.ds(lo, n)]

    def z_copy(w, src, dst, way, step, yy):
        return rdma(src, dst, z_s.at[w], z_r.at[w, way, step, yy], zp if way == 0 else zm)

    def keep_own(w):
        return pltpu.make_async_copy(own_part(w), w_rows(w, z, yl), loc.at[10 + w])

    def z_begin(w):
        lo, n = W_PARTS[w]
        ag4(str(w))
        w_own[lo : lo + n] = (wsh_0, wsh_1)[w][by_core(source)]
        rdma(own_part(w), w_rows(w, z, yl), zy_s.at[w], zy_r.at[w], yp).start()
        for way in (0, 1):
            z_copy(w, own_part(w), w_rows(w, z, yl), way, 0, yl).start()
        keep_own(w).start()

    def zag(w, step):
        if step == 0:
            ref = w_rows(w, z, 1 - yl)
            rdma(ref, ref, zy_s.at[w], zy_r.at[w], yp).wait_recv()
            for way in (0, 1):
                z_copy(w, ref, ref, way, 0, 1 - yl).start()
            return
        for way in (0, 1):
            zz = z - step if way == 0 else z + step
            if step == 1:
                for yy in (0, 1):
                    ref = w_rows(w, zz, yy)
                    z_copy(w, ref, ref, way, 0, yy).wait_recv()
            else:
                ref = w_pair(w, zz) if step < 4 else w_rows(w, zz, way)
                z_copy(w, ref, ref, way, step - 1, 0).wait_recv()
            if step < 4:
                ref = w_pair(w, zz) if step < 3 else w_rows(w, zz, way)
                z_copy(w, ref, ref, way, step, 0).start()

    z_begin(0)
    ag1(0)
    ag0(1)
    swap_far(0, hid_send)
    zag(0, 0)
    loads[1].wait()

    def perm_w(c, _):
        sel = chooser(c)
        for q in range(4):
            w_perm[c, :, q * 128 : (q + 1) * 128] = dot(
                w_res[:, q * 640 : (q + 1) * 640], sel, 1, 0
            ).astype(BF16)
        return 0

    ag3("1")
    lax.fori_loop(0, 2, perm_w, 0)
    ag2(0)
    z_begin(1)
    ag1(1)
    swap_near(0, hid_send, hid_in)
    lax.fori_loop(2, CHUNKS, perm_w, 0)
    ag3(0)
    zag(0, 1)
    zag(1, 0)
    acc[...] = jnp.zeros_like(acc)
    ag2(1)
    swap_pass(0, hid_in)
    ag0(2)

    def c_rows(c, zz, h=None):
        start = pl.multiple_of(((zz + 16) % 8) * 64 + (0 if h is None else h * 32), 32)
        return part.at[c, pl.ds(start, 64 if h is None else 32)]

    def add_into(ref, other_ref):
        ref[...] = (ref[...].astype(F32) + other_ref[...].astype(F32)).astype(BF16)

    def rs_move(c, step, way, src, dst):
        return rdma(src, dst, c_s.at[c], c_r.at[c, step, way], zp if way == 0 else zm)

    def rs(c, step):
        if step == 0:
            rs_move(c, 0, 0, c_rows(c, z + 4, 0), rs_r0.at[c]).start()
            rs_move(c, 0, 1, c_rows(c, z - 4, 1), rs_l0.at[c]).start()
            return
        if step == 5:
            rdma(yrecv.at[c], yrecv.at[c], cy_s.at[c], cy_r.at[c], yp).wait_recv()
            tot = eg_sum[c] + yrecv[c].astype(F32)
            eg_out[pl.ds(pl.multiple_of(c * 32, 32), 32), :] = (tot / 16.0).astype(BF16)
            return
        if step == 4:
            rs_move(c, 3, 0, rs_r.at[c, 2], rs_r.at[c, 2]).wait_recv()
            rs_move(c, 3, 1, rs_l.at[c, 2], rs_l.at[c, 2]).wait_recv()
            for h in (0, 1):
                rows = pl.ds(h * 32, 32)
                tot = (
                    c_rows(c, z, h)[...].astype(F32)
                    + rs_r[c, 2, rows, :].astype(F32)
                    + rs_l[c, 2, rows, :].astype(F32)
                )

                @pl.when(yl == h)
                def _():
                    eg_sum[c] = tot

                @pl.when(yl != h)
                def _():
                    ysend[c] = tot.astype(BF16)

            rdma(ysend.at[c], yrecv.at[c], cy_s.at[c], cy_r.at[c], yp).start()
            return
        for way, first, later in ((0, rs_r0, rs_r), (1, rs_l0, rs_l)):
            tgt = z + 4 - step if way == 0 else z - 4 + step
            if step == 1:
                rs_move(c, 0, way, first.at[c], first.at[c]).wait_recv()
                add_into(c_rows(c, tgt, way), first.at[c])
            else:
                rs_move(c, step - 1, way, later.at[c, step - 2], later.at[c, step - 2]).wait_recv()
                add_into(c_rows(c, tgt), later.at[c, step - 2])
            rs_move(c, step, way, c_rows(c, tgt), later.at[c, step - 1]).start()

    def rs_drain(c):
        ref = part.at[c, pl.ds(0, 2 * (32 + 3 * 64))]
        rdma(ref, ref, c_s.at[c], c_r.at[c, 0, 0], zp).wait_send()
        rdma(ysend.at[c], ysend.at[c], cy_s.at[c], cy_r.at[c], yp).wait_send()

    code_row = lax.broadcasted_iota(jnp.int32, (64, 128), 0).astype(F32)

    def place_rows():
        for s in range(ep_n):
            sel = (code_row == meta_in[s, 1:2, :]).astype(BF16)
            hid_rows[by_core(s)] = dot(sel, hid_in[s], 0, 0).astype(BF16)


    def back(c):
        def body(i, _):
            rows = pl.ds(i * 8, 8)
            res = dot(gat[c, rows].reshape(1024, 512), w_perm[c], 1, 1)
            acc[rows] += res.reshape(8, 128, width_h)
            return 0

        lax.fori_loop(0, 2, body, 0)

    def pack_back(first):
        for t in range(8):
            e = first + t
            sel = (code_row == meta_in[e, 0:1, :]).astype(BF16)
            ret_send[e] = dot(sel, acc[by_core(e)].astype(BF16), 1, 0).astype(BF16)

    def weight_part(c):
        def body(n, _):
            rows = pl.ds(pl.multiple_of(n * 256, 256), 256)
            left_rows = gat[c, :, :, rows].reshape(ep_n * 128, 256)
            part[c, rows] = dot(left_rows, hid_rows[...].reshape(ep_n * 128, width_h), 0, 0).astype(BF16)
            return 0

        lax.fori_loop(0, 2, body, 0)

    def inside(c, f):
        pl.when((c >= 0) & (c < CHUNKS))(lambda: f(c))

    def sums(i):
        for step in (4, 3, 2, 1):
            inside(i - step, lambda c: rs(c, step))

    ag4(0)
    back(0)
    zag(0, 2)
    ag3(1)
    ag1(2)
    zag(1, 1)
    ag4(1)
    back(1)
    zag(0, 3)
    ag0(3)
    ag2(2)
    spread_wait(meta_in, meta_s, meta_r)
    swap_wait(0, hid_in)
    place_rows()
    weight_part(0)
    rs(0, 0)
    ag3(2)
    ag1(3)
    ag0(4)
    zag(1, 2)
    weight_part(1)
    rs(1, 0)
    rs(0, 1)

    def tick(i, _):
        inside(i + 1, ag2)
        inside(i + 2, ag1)
        ag4(i)
        back(i)
        sums(i)
        weight_part(i)
        rs(i, 0)
        inside(i + 1, ag3)
        pl.when(i == 2)(lambda: zag(1, 3))
        return 0

    lax.fori_loop(2, CHUNKS - 1, tick, 0)

    last = CHUNKS - 1
    ag4(last)
    back(last)
    weight_part(last)
    rs(last, 0)
    pack_back(far)
    swap_far(1, ret_send)
    sums(last)
    pack_back(near)
    swap_near(1, ret_send, ret_in)

    def tail(i, _):
        sums(i)
        return 0

    lax.fori_loop(CHUNKS, CHUNKS + 2, tail, 0)
    swap_pass(1, ret_in)
    lax.fori_loop(CHUNKS + 2, CHUNKS + 4, tail, 0)
    for c in range(CHUNKS):
        rs(c, 5)
    swap_wait(1, ret_in)
    keep_ret = pltpu.make_async_copy(ret_in, ret_out, loc.at[12])
    keep_ret.start()
    zag(0, 4)
    zag(1, 4)

    ag_drain("0")
    ag_drain("1")

    def drain(c, _):
        ag_drain(c)
        rs_drain(c)
        return 0

    lax.fori_loop(0, CHUNKS, drain, 0)
    spread_drain(meta_send, meta_s, meta_r)
    swap_drain(0)
    swap_drain(1)
    for w in (0, 1):
        keep_own(w).wait()
        rdma(own_part(w), own_part(w), zy_s.at[w], zy_r.at[w], yp).wait_send()
        lo, n = W_PARTS[w]
        sent = w_out.at[pl.ds(0, 7), :, pl.ds(lo, n)]
        z_copy(w, sent, sent, 0, 0, 0).wait_send()
    keep_ret.wait()


def finish(ret_h, rows_at, gates, w_in, eg_in, sg_out, w_out, eg_out, ret, w_v, sg_v, sems):
    load = pltpu.make_async_copy(ret_h, ret, sems.at[24])
    load.start()
    pieces = 12
    n = w_in.shape[0] // pieces
    rows_of = [pl.ds(p * n, n) for p in range(pieces)]
    ups = [pltpu.make_async_copy(w_in.at[r], w_v.at[r], sems.at[p]) for p, r in enumerate(rows_of)]
    downs = [pltpu.make_async_copy(w_v.at[r], w_out.at[r], sems.at[pieces + p]) for p, r in enumerate(rows_of)]
    for cp in ups:
        cp.start()
    eg_out[...] = eg_in[...]
    load.wait()
    outs = []
    rows = lax.broadcasted_iota(jnp.int32, (1024, 128), 0).astype(F32)
    for k in range(6):
        for p in range(k * pieces // 6, (k + 1) * pieces // 6):
            ups[p].wait()
            downs[p].start()
        both = gates[k]
        gate = jnp.concatenate([both[0:1], both[1:2]], axis=1)
        sel = jnp.where(rows == rows_at[k : k + 1, :], gate, 0.0).astype(BF16)
        got = dot(sel, ret[...].reshape(1024, ret.shape[-1]), 0, 0).astype(BF16)
        sg_v[k] = got.reshape(2, 64, got.shape[-1])
        outs.append(pltpu.make_async_copy(sg_v.at[k], sg_out.at[:, k], sems.at[25 + k]))
        outs[-1].start()
    for cp in downs + outs:
        cp.wait()


def local(expert_ids, gates, hidden, cotangent, old_place, new_place, old_weights):
    micros, toks, tops = expert_ids.shape
    width_h, width_d = old_weights.shape[1:]
    lanes = micros * toks
    share = width_h // 16
    out_rows = width_d // 16
    ids_t = expert_ids.transpose(2, 0, 1)
    gates_t = gates.transpose(2, 0, 1)
    hid_t = hidden.transpose(0, 2, 1, 3)
    cot = cotangent.reshape(lanes, width_d)
    vmem, smem, hbm = (pl.BlockSpec(memory_space=m) for m in (pltpu.VMEM, pltpu.SMEM, pl.ANY))
    dma = pltpu.SemaphoreType.DMA
    v = pltpu.VMEM
    cw = width_d // CHUNKS
    scratch = [
        v((CHUNKS, 16, lanes, cw), BF16),
        v((16, W_PARTS[0][1], width_d), BF16),
        v((16, W_PARTS[1][1], width_d), BF16),
        v((width_h, width_d), BF16),
        v((CHUNKS, width_h, cw), BF16),
        v((lanes, width_d), BF16),
        v((tops, micros, toks, width_h), BF16),
        v((16 * micros * CAP, tops * lanes), BF16),
        v((16, micros * CAP, width_h), BF16),
        v((16, micros * CAP, width_h), BF16),
        v((16, lanes, width_h), BF16),
        v((16, lanes, width_h), F32),
        v((16, 8, lanes), F32),
        v((16, 8, lanes), F32),
        v((16, micros * CAP, width_h), BF16),
        v((16, micros * CAP, width_h), BF16),
        v((CHUNKS, cw, width_h), BF16),
        v((CHUNKS, 32, width_h), BF16),
        v((CHUNKS, 32, width_h), BF16),
        v((CHUNKS, 3, 64, width_h), BF16),
        v((CHUNKS, 3, 64, width_h), BF16),
        v((CHUNKS, 32, width_h), BF16),
        v((CHUNKS, 32, width_h), BF16),
        v((CHUNKS, 32, width_h), F32),
        v((share, width_d), BF16),
        v((2, 8, CAP, width_h), BF16),
        v((2, 8, CAP, width_h), BF16),
        dma((13,)),
        dma((CHUNKS + 2,)),
        dma((CHUNKS + 2, PIECES)),
        dma((1,)), dma((5,)),
        dma((1,)), dma((1,)),
        dma((1,)), dma((5,)),
        dma((2,)), dma((2, 2, 4, 2)),
        dma((2,)), dma((2,)),
        dma((CHUNKS,)), dma((CHUNKS, 4, 2)),
        dma((CHUNKS,)), dma((CHUNKS,)),
    ]
    ret, rows_at, weights, grads = pl.pallas_call(
        kernel,
        out_shape=(
            jax.ShapeDtypeStruct((16, micros * CAP, width_h), BF16),
            jax.ShapeDtypeStruct((8, lanes), F32),
            jax.ShapeDtypeStruct((8, 2, share, width_d), BF16),
            jax.ShapeDtypeStruct((out_rows, width_h), BF16),
        ),
        in_specs=[vmem, vmem, smem, smem, hbm, hbm, hbm],
        out_specs=(hbm, vmem, hbm, vmem),
        scratch_shapes=scratch,
        compiler_params=pltpu.CompilerParams(
            collective_id=0, has_side_effects=True, vmem_limit_bytes=60 * 1024 * 1024
        ),
    )(ids_t, gates_t, old_place, new_place, hid_t, cot, old_weights[0])
    weights = weights.reshape(width_h, width_d)
    slot_grads, new_weights, grads = pl.pallas_call(
        finish,
        out_shape=(
            jax.ShapeDtypeStruct(hid_t.shape, BF16),
            jax.ShapeDtypeStruct(weights.shape, BF16),
            jax.ShapeDtypeStruct(grads.shape, BF16),
        ),
        in_specs=[hbm, vmem, vmem, hbm, vmem],
        out_specs=(hbm, hbm, vmem),
        scratch_shapes=[
            v(ret.shape, BF16),
            v(weights.shape, BF16),
            v((tops, micros, toks, width_h), BF16),
            dma((31,)),
        ],
        compiler_params=pltpu.CompilerParams(vmem_limit_bytes=60 * 1024 * 1024),
    )(ret, rows_at, gates_t, weights, grads)
    return slot_grads.transpose(0, 2, 1, 3), new_weights[None], grads.T[None]


def solution(mesh):
    in_specs = (
        P(None, ("grp", "ep"), None),
        P(None, ("grp", "ep"), None),
        P(None, ("grp", "ep"), None, None),
        P(None, ("grp", "ep"), None),
        P(),
        P(),
        P("ep", None, None),
    )
    out_specs = (P(None, ("grp", "ep"), None, None), P("ep", None, None), P("ep", None, "grp"))
    return jax.shard_map(local, mesh=mesh, in_specs=in_specs, out_specs=out_specs, check_vma=False)
```
